32 devices in a mesh: cohort: 2 (over x), region: 16 (over z, y, core).
Axes of the slice: x: 2, y: 2, z: 4, core: 2. Of those that a mesh axis runs over, the one named last changes fastest.
Arguments:
- dosage: bfloat16 [4096, 16384], P('cohort', 'region'), parts along dimension 0, may hold values from 0 to 2, as said below
- eigvec: bfloat16 [16384, 2048], P('region', 'cohort'), parts along dimension 1, may hold values from -1 to 1, as said below
- eigval: float32 [2, 16384], P('cohort', 'region'), parts along dimension 0, may hold values from 64 to 65536
- pheno: bfloat16 [4096, 128], P('cohort'), parts along dimension 0, may hold values from 0 to 1, as said below
Outputs:
- level1_weights: float32 [128, 128], P('region', 'cohort'), parts along dimension 1
The draws below stay inside these ranges and needn't reach their ends.
There are 2 independent parts, one for each index of `cohort`. The reference program is written for one: setup_inputs(seed, part) draws one part's arguments, and reference() takes and returns one part's arrays. A program takes and returns all parts, laid end to end along the dimension named above; each array names one. Nothing has to cross between parts.
Inputs may be any that keep to these rules, and one draw needn't show every extreme that they name: Every entry is a whole dosage 0, 1 or 2. `eigvec`: the rows of each block form an orthonormal basis up to rounding. `pheno`: every entry is 0 or 1.
All inputs are finite; a program needn't handle non-finite values.
Results may differ from the reference program's by a relative error of at most 0.0051.
Values may be sent and summed in bfloat16 or wider, within the bound.
A program may use at most 64 MiB of HBM per device.

```python
import math
import jax
import jax.numpy as jnp
from jax import lax

BLK = 1024
TRAITS = 128
SAMPLES = 2048
NEWTON = 3
VARIANTS = 16384


def draw_dosage(key, part):
    freq = jax.random.randint(jax.random.fold_in(key, 11), (1, VARIANTS), 100, 501)
    first = jax.random.randint(jax.random.fold_in(key, 12), (SAMPLES, VARIANTS), 0, 1000)
    second = jax.random.randint(jax.random.fold_in(key, 13), (SAMPLES, VARIANTS), 0, 1000)
    count = (first < freq).astype(jnp.int32) + (second < freq).astype(jnp.int32)
    return count.astype(jnp.float32).astype(jnp.bfloat16)


def draw_eigvec(key, part):
    blocks = VARIANTS // BLK
    normal = jax.random.normal(jax.random.fold_in(key, 21), (blocks, BLK, BLK), jnp.float32)
    basis, upper = jnp.linalg.qr(normal)
    return basis.reshape(VARIANTS, BLK).astype(jnp.bfloat16)


def draw_pheno(key, part):
    status = jax.random.randint(jax.random.fold_in(key, 31), (SAMPLES, TRAITS), 0, 2)
    return status.astype(jnp.float32).astype(jnp.bfloat16)


def shard_levels(stream_key, extent, cuts, smallest, largest):
    def one(dim, parts):
        steps = jax.random.uniform(jax.random.fold_in(jax.random.fold_in(stream_key, 6), dim), (parts,), jnp.float32, smallest / len(cuts), largest / len(cuts))
        return jnp.repeat(jnp.exp(steps), extent[dim] // parts).reshape((-1,) + (1,) * (len(extent) - dim - 1))

    loudness = one(*cuts[0])
    for cut in cuts[1:]:
        loudness = loudness * one(*cut)
    return loudness


def setup_inputs(seed: int = 0, part: int = 0) -> dict:
    seeds = jax.random.split(jax.random.key(seed), 5)
    part_splits = jax.random.split(jax.random.fold_in(seeds[4], part), 5)
    dosage = draw_dosage(jax.random.fold_in(jax.random.fold_in(seeds[4], part), 71), part)
    eigvec = draw_eigvec(jax.random.fold_in(jax.random.fold_in(seeds[4], part), 71), part)
    eigval = jnp.clip(jnp.exp(math.log(65536.0) - 6.931472 * jax.random.uniform(part_splits[2], (1, VARIANTS), jnp.float32) ** shard_levels(part_splits[2], (1, VARIANTS), ((1, 16),), -0.2, 0.2)), 64.0, 65536.0)
    pheno = draw_pheno(jax.random.fold_in(jax.random.fold_in(seeds[4], part), 71), part)
    return dict(dosage=dosage, eigvec=eigvec, eigval=eigval, pheno=pheno)


EPSILON = 1e-05
HERITABILITY = (0.01, 0.25, 0.75, 0.99)
LEVEL_ONE = 0.03125

def standardize(values):
    values = values.astype(jnp.float32)
    center = lax.optimization_barrier(jnp.mean(values, axis=0))
    spread = jnp.sqrt(lax.optimization_barrier(jnp.mean(jnp.square(values - center), axis=0)) + EPSILON)
    return ((values - center) / spread).astype(jnp.bfloat16)

def fit_trait(operands):
    design, target = operands
    predictors = design.shape[0]
    level_ridge = LEVEL_ONE * design.shape[1]
    weights = jnp.zeros((predictors,), jnp.float32)
    identity = jnp.eye(predictors, dtype=jnp.float32)
    for newton_step in range(NEWTON):
        logits = jnp.dot(weights.astype(jnp.bfloat16).astype(jnp.float32), design.astype(jnp.float32), preferred_element_type=jnp.float32)
        prob = jax.nn.sigmoid(logits)
        resid = (target - prob).astype(jnp.bfloat16)
        weighted = (design.astype(jnp.float32) * (prob * (1.0 - prob))).astype(jnp.bfloat16)
        gram = jnp.dot(weighted.astype(jnp.float32), design.T.astype(jnp.float32), preferred_element_type=jnp.float32)
        grad = jnp.dot(design.astype(jnp.float32), resid.astype(jnp.float32), preferred_element_type=jnp.float32) - level_ridge * weights
        factor = jnp.linalg.cholesky(gram + level_ridge * identity)
        partial_solve = lax.linalg.triangular_solve(factor, grad[:, None], left_side=True, lower=True)
        update = lax.linalg.triangular_solve(factor, partial_solve, left_side=True, lower=True, transpose_a=True)
        weights = weights + update[:, 0]
    return weights

def reference(dosage, eigvec, eigval, pheno):
    samples = dosage.shape[0]
    blocks = VARIANTS // BLK
    ridges = len(HERITABILITY)
    shrink = jnp.array([BLK * (1.0 - value) / value for value in HERITABILITY], jnp.float32)
    std_trait = standardize(pheno)
    geno_blocks = dosage.reshape(samples, blocks, BLK).transpose(1, 0, 2)
    bases = eigvec.reshape(blocks, BLK, BLK)
    values = eigval.reshape(blocks, BLK)

    def level_zero(operands):
        genotype, basis, spectrum = operands
        std_geno = standardize(genotype)
        cross = lax.dot_general(std_geno.astype(jnp.float32), std_trait.astype(jnp.float32), (((0,), (0,)), ((), ())), preferred_element_type=jnp.float32).astype(jnp.bfloat16)
        rotated = lax.dot_general(basis.astype(jnp.float32), cross.astype(jnp.float32), (((0,), (0,)), ((), ())), preferred_element_type=jnp.float32)
        scaled = (rotated[:, None, :] / (spectrum[:, None, None] + shrink[None, :, None])).astype(jnp.bfloat16)
        ridge = jnp.dot(basis.astype(jnp.float32), scaled.reshape(BLK, ridges * TRAITS).astype(jnp.float32), preferred_element_type=jnp.float32).astype(jnp.bfloat16)
        predicted = lax.dot_general(ridge.astype(jnp.float32), std_geno.astype(jnp.float32), (((0,), (1,)), ((), ())), preferred_element_type=jnp.float32).astype(jnp.bfloat16)
        return predicted.reshape(ridges, TRAITS, samples)
    predictions = lax.map(level_zero, (geno_blocks, bases, values))
    design = predictions.transpose(2, 1, 0, 3).reshape(TRAITS, ridges * blocks, samples)
    target = pheno.astype(jnp.float32).T
    return lax.map(fit_trait, (design, target))
```

```python
import functools

import jax
import jax.numpy as jnp
from jax import lax
from jax.experimental import pallas as pl
from jax.experimental.pallas import tpu as pltpu
from jax.sharding import PartitionSpec as P

NEWTON = 3


EPSILON = 1e-05
HERITABILITY = (0.01, 0.25, 0.75, 0.99)
LEVEL_ONE = 0.03125
LANES = 128
ROWS = 8


def standardize(values):
    values = values.astype(jnp.float32)
    center = jnp.mean(values, axis=0)
    spread = jnp.sqrt(jnp.mean(jnp.square(values - center), axis=0) + EPSILON)
    return ((values - center) / spread).astype(jnp.bfloat16)


def pick_column(matrix, column, width):
    lane = lax.broadcasted_iota(jnp.int32, matrix.shape, 1)
    if matrix.shape[1] == LANES:
        return jnp.take_along_axis(matrix, lane // width * width + column, axis=1)
    chosen = jnp.sum(jnp.where(lane == column, matrix, 0.0), axis=1, keepdims=True)
    return jnp.broadcast_to(chosen, matrix.shape)


def eliminate(curve_ref, slope_ref, width):
    groups = curve_ref.shape[0]
    lanes = curve_ref.shape[2]
    row = lax.broadcasted_iota(jnp.int32, (ROWS, lanes), 0)

    def panel(step, carry):
        first = pl.multiple_of(step * ROWS, ROWS)
        curves = [curve_ref[g, pl.ds(first, ROWS), :] for g in range(groups)]
        slopes = [slope_ref[g, pl.ds(first, ROWS), :] for g in range(groups)]
        for j in range(ROWS):
            for g in range(groups):
                column = pick_column(curves[g], first + j, width)
                inverse = 1.0 / column[j : j + 1, :]
                pivot = curves[g][j : j + 1, :] * inverse
                right = slopes[g][j : j + 1, :] * inverse
                curves[g] = jnp.where(row == j, pivot, curves[g] - column * pivot)
                slopes[g] = jnp.where(row == j, right, slopes[g] - column * right)
        for g in range(groups):
            old = curve_ref[g]
            curve = old
            slope = slope_ref[g]
            for j in range(ROWS):
                column = pick_column(old, first + j, width)
                curve = curve - column * curves[g][j : j + 1, :]
                slope = slope - column * slopes[g][j : j + 1, :]
            curve_ref[g] = curve
            slope_ref[g] = slope
        for g in range(groups):
            curve_ref[g, pl.ds(first, ROWS), :] = curves[g]
            slope_ref[g, pl.ds(first, ROWS), :] = slopes[g]
        return carry

    lax.fori_loop(0, width // ROWS, panel, 0)


def spread_weights(weight_ref, chunk, width, count, pack):
    lane = lax.broadcasted_iota(jnp.int32, (width, LANES), 1)
    parts = []
    for t in range(count):
        group, half = divmod(chunk * count + t, pack)
        held = weight_ref[group][:, :LANES]
        if half:
            held = pltpu.roll(held, LANES - half * width, 1)
        parts.append(jnp.where(lane == t, held, 0.0))
    return jnp.concatenate(parts, axis=0).T[:ROWS, :]


def fit_kernel(width, design_ref, target_ref, out_ref, curve_ref, slope_ref, weight_ref):
    chunks, rows, samples = design_ref.shape
    count = rows // width
    lanes = curve_ref.shape[2]
    pack = lanes // width
    tile = 512
    ridge = LEVEL_ONE * samples
    weight_ref[...] = jnp.zeros_like(weight_ref)
    lane = lax.broadcasted_iota(jnp.int32, (width, lanes), 1)
    row = lax.broadcasted_iota(jnp.int32, (width, lanes), 0)
    identity = jnp.where(lane % width == row, ridge, 0.0)

    def newton(step, carry):
        for chunk in range(chunks):
            weights = spread_weights(weight_ref, chunk, width, count, pack).astype(jnp.bfloat16)
            gram = jnp.zeros((rows, rows), jnp.float32)
            grad = jnp.zeros((rows, ROWS), jnp.float32)
            for first in range(0, samples, tile):
                design = design_ref[chunk, :, first : first + tile]
                logits = jnp.dot(weights, design, preferred_element_type=jnp.float32)
                prob = 1.0 / (1.0 + jnp.exp(-logits))
                resid = (target_ref[chunk, :, first : first + tile] - prob).astype(jnp.bfloat16)
                curve = prob * (1.0 - prob)
                weighted = jnp.concatenate(
                    [
                        (
                            design[t * width : (t + 1) * width].astype(jnp.float32)
                            * curve[t : t + 1, :]
                        ).astype(jnp.bfloat16)
                        for t in range(count)
                    ],
                    axis=0,
                )
                last = (((1,), (1,)), ((), ()))
                gram += lax.dot_general(weighted, design, last, preferred_element_type=jnp.float32)
                grad += lax.dot_general(design, resid, last, preferred_element_type=jnp.float32)
            for own in range(count // pack):
                group = chunk * count // pack + own
                curve = None
                for half in range(pack):
                    t = own * pack + half
                    part = gram[t * width : (t + 1) * width, own * lanes : (own + 1) * lanes]
                    side = jnp.broadcast_to(
                        grad[t * width : (t + 1) * width, t : t + 1], (width, lanes)
                    )
                    if curve is None:
                        curve, slope = part, side
                    else:
                        curve = jnp.where(lane < half * width, curve, part)
                        slope = jnp.where(lane < half * width, slope, side)
                curve_ref[group] = curve + identity
                slope_ref[group] = slope - ridge * weight_ref[group]
        eliminate(curve_ref, slope_ref, width)
        weight_ref[...] += slope_ref[...]
        return carry

    lax.fori_loop(0, NEWTON, newton, 0)
    for chunk in range(chunks):
        out_ref[chunk] = spread_weights(weight_ref, chunk, width, count, pack)


def fit_traits(moved, target):
    traits, samples = target.shape
    design = jnp.moveaxis(moved, 1, 0).reshape(traits, -1, samples)
    width = design.shape[1]
    lanes = max(width, LANES)
    count = max(1, 2 * LANES // width)
    chunks = traits // count
    groups = traits * width // lanes
    target = jnp.pad(
        target.reshape(chunks, count, samples), ((0, 0), (0, ROWS - count), (0, 0))
    )
    weights = pl.pallas_call(
        functools.partial(fit_kernel, width),
        out_shape=jax.ShapeDtypeStruct((chunks, ROWS, count * width), jnp.float32),
        in_specs=[pl.BlockSpec(memory_space=pltpu.VMEM)] * 2,
        out_specs=pl.BlockSpec(memory_space=pltpu.VMEM),
        scratch_shapes=[pltpu.VMEM((groups, width, lanes), jnp.float32)] * 3,
        compiler_params=pltpu.CompilerParams(vmem_limit_bytes=48 * 2**20),
        name="newton",
    )(design.reshape(chunks, count * width, samples), target)
    return jnp.sum(weights, axis=1).reshape(traits, width)


def on_device(dosage, eigvec, eigval, pheno):
    samples, width = dosage.shape
    traits = pheno.shape[1]
    regions = lax.axis_size("region")
    ridges = len(HERITABILITY)
    per_device = traits // regions
    shrink = jnp.array([width * (1.0 - value) / value for value in HERITABILITY], jnp.float32)
    std_trait = standardize(pheno)
    std_geno = standardize(dosage)
    cross = lax.dot_general(
        std_geno, std_trait, (((0,), (0,)), ((), ())), preferred_element_type=jnp.float32
    ).astype(jnp.bfloat16)
    rotated = lax.dot_general(
        eigvec, cross, (((0,), (0,)), ((), ())), preferred_element_type=jnp.float32
    )
    scaled = (rotated[:, None, :] / (eigval[0][:, None, None] + shrink[None, :, None])).astype(
        jnp.bfloat16
    )
    ridge = jnp.dot(
        eigvec, scaled.reshape(width, ridges * traits), preferred_element_type=jnp.float32
    ).astype(jnp.bfloat16)
    position = lax.axis_index("region")
    predicted = lax.dot_general(
        ridge, std_geno, (((0,), (1,)), ((), ())), preferred_element_type=jnp.float32
    ).astype(jnp.bfloat16)
    predicted = predicted.reshape(ridges, traits, 1, samples)
    moved = lax.all_to_all(predicted, "region", split_axis=1, concat_axis=2, tiled=True)
    target = lax.dynamic_slice_in_dim(pheno, position * per_device, per_device, 1)
    return fit_traits(moved, target.astype(jnp.float32).T)


def solution(mesh):
    return jax.shard_map(
        on_device,
        mesh=mesh,
        in_specs=(
            P("cohort", "region"),
            P("region", "cohort"),
            P("cohort", "region"),
            P("cohort", None),
        ),
        out_specs=P("region", "cohort"),
        check_vma=False,
    )
```

```python
import functools

import jax
import jax.numpy as jnp
from jax import lax
from jax.experimental import pallas as pl
from jax.experimental.pallas import tpu as pltpu
from jax.sharding import PartitionSpec as P

NEWTON = 3


EPSILON = 1e-05
HERITABILITY = (0.01, 0.25, 0.75, 0.99)
LEVEL_ONE = 0.03125
LANES = 128
ROWS = 8


def pick_column(matrix, column, width):
    lane = lax.broadcasted_iota(jnp.int32, matrix.shape, 1)
    if matrix.shape[1] == LANES:
        return jnp.take_along_axis(matrix, lane // width * width + column, axis=1)
    chosen = jnp.sum(jnp.where(lane == column, matrix, 0.0), axis=1, keepdims=True)
    return jnp.broadcast_to(chosen, matrix.shape)


def eliminate(curve_ref, slope_ref, width):
    groups = curve_ref.shape[0]
    lanes = curve_ref.shape[2]
    row = lax.broadcasted_iota(jnp.int32, (ROWS, lanes), 0)

    def panel(step, carry):
        first = pl.multiple_of(step * ROWS, ROWS)
        curves = [curve_ref[g, pl.ds(first, ROWS), :] for g in range(groups)]
        slopes = [slope_ref[g, pl.ds(first, ROWS), :] for g in range(groups)]
        for j in range(ROWS):
            for g in range(groups):
                column = pick_column(curves[g], first + j, width)
                inverse = 1.0 / column[j : j + 1, :]
                pivot = curves[g][j : j + 1, :] * inverse
                right = slopes[g][j : j + 1, :] * inverse
                curves[g] = jnp.where(row == j, pivot, curves[g] - column * pivot)
                slopes[g] = jnp.where(row == j, right, slopes[g] - column * right)
        for g in range(groups):
            old = curve_ref[g]
            curve = old
            slope = slope_ref[g]
            for j in range(ROWS):
                column = pick_column(old, first + j, width)
                curve = curve - column * curves[g][j : j + 1, :]
                slope = slope - column * slopes[g][j : j + 1, :]
            curve_ref[g] = curve
            slope_ref[g] = slope
        for g in range(groups):
            curve_ref[g, pl.ds(first, ROWS), :] = curves[g]
            slope_ref[g, pl.ds(first, ROWS), :] = slopes[g]
        return carry

    lax.fori_loop(0, width // ROWS, panel, 0)


def spread_weights(weight_ref, chunk, width, count, pack):
    lane = lax.broadcasted_iota(jnp.int32, (width, LANES), 1)
    parts = []
    for t in range(count):
        group, half = divmod(chunk * count + t, pack)
        held = weight_ref[group][:, :LANES]
        if half:
            held = pltpu.roll(held, LANES - half * width, 1)
        parts.append(jnp.where(lane == t, held, 0.0))
    return jnp.concatenate(parts, axis=0).T[:ROWS, :]


def fit(width, target_chunk, design_ref, target_ref, curve_ref, slope_ref, weight_ref):
    chunks, rows, samples = design_ref.shape
    count = rows // width
    lanes = curve_ref.shape[2]
    pack = lanes // width
    tile = 512
    ridge = LEVEL_ONE * samples
    weight_ref[...] = jnp.zeros_like(weight_ref)
    lane = lax.broadcasted_iota(jnp.int32, (width, lanes), 1)
    row = lax.broadcasted_iota(jnp.int32, (width, lanes), 0)
    identity = jnp.where(lane % width == row, ridge, 0.0)

    def newton(step, carry):
        for chunk in range(chunks):
            weights = spread_weights(weight_ref, chunk, width, count, pack).astype(jnp.bfloat16)
            gram = jnp.zeros((rows, rows), jnp.float32)
            grad = jnp.zeros((rows, ROWS), jnp.float32)
            for first in range(0, samples, tile):
                design = design_ref[chunk, :, first : first + tile]
                logits = jnp.dot(weights, design, preferred_element_type=jnp.float32)
                prob = 1.0 / (1.0 + jnp.exp(-logits))
                target = target_ref[target_chunk + chunk, :, first : first + tile]
                resid = (target - prob).astype(jnp.bfloat16)
                curve = prob * (1.0 - prob)
                weighted = jnp.concatenate(
                    [
                        (
                            design[t * width : (t + 1) * width].astype(jnp.float32)
                            * curve[t : t + 1, :]
                        ).astype(jnp.bfloat16)
                        for t in range(count)
                    ],
                    axis=0,
                )
                gram += dot_last(weighted, design)
                grad += dot_last(design, resid)
            for own in range(count // pack):
                group = chunk * count // pack + own
                curve = None
                for half in range(pack):
                    t = own * pack + half
                    part = gram[t * width : (t + 1) * width, own * lanes : (own + 1) * lanes]
                    side = jnp.broadcast_to(
                        grad[t * width : (t + 1) * width, t : t + 1], (width, lanes)
                    )
                    if curve is None:
                        curve, slope = part, side
                    else:
                        curve = jnp.where(lane < half * width, curve, part)
                        slope = jnp.where(lane < half * width, slope, side)
                curve_ref[group] = curve + identity
                slope_ref[group] = slope - ridge * weight_ref[group]
        eliminate(curve_ref, slope_ref, width)
        weight_ref[...] += slope_ref[...]
        return carry

    lax.fori_loop(0, NEWTON, newton, 0)


def dot_last(left, right):
    return lax.dot_general(
        left, right, (((1,), (1,)), ((), ())), preferred_element_type=jnp.float32
    )


def kernel(
    regions,
    dosage_ref,
    eigvec_ref,
    eigval_ref,
    pheno_ref,
    out_ref,
    geno_ref,
    trait_ref,
    std_trait_ref,
    cross_ref,
    wide_ref,
    scaled_ref,
    ridge_ref,
    sent_ref,
    held_ref,
    design_ref,
    target_ref,
    curve_ref,
    slope_ref,
    weight_ref,
    send_sem,
    recv_sem,
):
    samples, block = dosage_ref.shape
    traits = pheno_ref.shape[1]
    sends, _, piece, _ = sent_ref.shape
    chunks, rows, _ = design_ref.shape
    ridges = len(HERITABILITY)
    width = regions * ridges
    count = rows // width
    per_device = traits // regions
    per_send = per_device // sends
    tile = 256
    me = lax.axis_index("region")

    barrier = pltpu.get_barrier_semaphore()

    def greet(k, carry):
        other = lax.rem(me + k, regions)
        pl.semaphore_signal(
            barrier, inc=1, device_id={"region": other}, device_id_type=pl.DeviceIdType.MESH
        )
        return carry

    lax.fori_loop(1, regions, greet, 0)
    pl.semaphore_wait(barrier, regions - 1)

    trait = pheno_ref[...].astype(jnp.float32).T
    trait_ref[...] = trait
    center = jnp.mean(trait, axis=1, keepdims=True)
    spread = jnp.sqrt(jnp.mean(jnp.square(trait - center), axis=1, keepdims=True) + EPSILON)
    std_trait_ref[...] = ((trait - center) / spread).astype(jnp.bfloat16)
    target_ref[...] = jnp.zeros_like(target_ref)
    for t in range(per_device):
        target_ref[t // count, t % count : t % count + 1, :] = trait_ref[
            pl.ds(me * per_device + t, 1), :
        ]

    def totals(i, carry):
        first, second = carry
        part = dosage_ref[pl.ds(pl.multiple_of(i * tile, tile), tile), :].astype(jnp.float32)
        part = part.reshape(tile // ROWS, ROWS, block)
        return first + jnp.sum(part, axis=0), second + jnp.sum(part * part, axis=0)

    zero = jnp.zeros((ROWS, block), jnp.float32)
    first, second = lax.fori_loop(0, samples // tile, totals, (zero, zero))
    first = jnp.sum(first, axis=0, keepdims=True)
    second = jnp.sum(second, axis=0, keepdims=True)
    mean = first / samples
    variance = (samples * second - first * first) / (samples * samples)
    scale = 1.0 / jnp.sqrt(variance + EPSILON)
    cross_ref[...] = jnp.zeros_like(cross_ref)

    def normalize(i, carry):
        here = pl.ds(pl.multiple_of(i * tile, tile), tile)
        part = ((dosage_ref[here, :].astype(jnp.float32) - mean) * scale).astype(jnp.bfloat16)
        geno_ref[here, :] = part
        cross_ref[...] += jnp.dot(
            std_trait_ref[:, here], part, preferred_element_type=jnp.float32
        )
        return carry

    lax.fori_loop(0, samples // tile, normalize, 0)

    all_rows = traits * ridges
    place = lax.broadcasted_iota(jnp.int32, (all_rows, traits), 0)
    which = lax.broadcasted_iota(jnp.int32, (all_rows, traits), 1)
    source = (
        place // piece % regions * per_device
        + place // (piece * regions) * per_send
        + place % per_send
    )
    choose = jnp.where(source == which, 1.0, 0.0).astype(jnp.bfloat16)
    wide_ref[...] = jnp.dot(
        choose, cross_ref[...].astype(jnp.bfloat16), preferred_element_type=jnp.float32
    ).astype(jnp.bfloat16)
    kind = lax.broadcasted_iota(jnp.int32, (all_rows, tile), 0) // per_send % ridges
    shrink = jnp.zeros((all_rows, tile), jnp.float32)
    for r, value in enumerate(HERITABILITY):
        shrink = jnp.where(kind == r, block * (1.0 - value) / value, shrink)

    def rotate(i, carry):
        here = pl.ds(pl.multiple_of(i * tile, tile), tile)
        rotated = jnp.dot(wide_ref[...], eigvec_ref[:, here], preferred_element_type=jnp.float32)
        scaled_ref[:, here] = (rotated / (eigval_ref[:, here] + shrink)).astype(jnp.bfloat16)
        return carry

    lax.fori_loop(0, block // tile, rotate, 0)

    def back(i, carry):
        here = pl.ds(pl.multiple_of(i * tile, tile), tile)
        ridge_ref[:, here] = dot_last(scaled_ref[...], eigvec_ref[here, :]).astype(jnp.bfloat16)
        return carry

    lax.fori_loop(0, block // tile, back, 0)

    def copy(send, other, slot):
        return pltpu.make_async_remote_copy(
            src_ref=sent_ref.at[send, other],
            dst_ref=held_ref.at[send, slot],
            send_sem=send_sem.at[send, other],
            recv_sem=recv_sem.at[send, slot],
            device_id={"region": other},
            device_id_type=pl.DeviceIdType.MESH,
        )

    send_rows = regions * piece
    for send in range(sends):

        def predict(i, carry):
            here = pl.ds(pl.multiple_of(i * tile, tile), tile)
            part = dot_last(
                ridge_ref[send * send_rows : (send + 1) * send_rows, :], geno_ref[here, :]
            )
            part = part.astype(jnp.bfloat16).astype(sent_ref.dtype)
            sent_ref[send, :, :, here] = part.reshape(regions, piece, tile)
            return carry

        lax.fori_loop(0, samples // tile, predict, 0)

        def start(k, carry):
            offset = regions // 2 + (k + 1) // 2 * (1 - 2 * (k % 2))
            copy(send, lax.rem(me + offset, regions), me).start()
            return carry

        lax.fori_loop(0, regions - 1, start, 0)
        held_ref[send, me] = sent_ref[send, me]

    place = lax.broadcasted_iota(jnp.int32, (send_rows, send_rows), 0)
    which = lax.broadcasted_iota(jnp.int32, (send_rows, send_rows), 1)
    wanted = which % per_send * width + which // per_send % ridges * regions + which // piece
    order = jnp.where(place == wanted, 1.0, 0.0).astype(jnp.bfloat16)
    for send in range(sends):

        def arrive(k, carry):
            other = lax.rem(me + k, regions)
            copy(send, other, other).wait_recv()
            return carry

        lax.fori_loop(1, regions, arrive, 0)

        def sort(i, carry):
            here = pl.ds(pl.multiple_of(i * tile, tile), tile)
            part = held_ref[send, :, :, here].reshape(send_rows, tile).astype(jnp.bfloat16)
            part = jnp.dot(order, part, preferred_element_type=jnp.float32).astype(jnp.bfloat16)
            design_ref[:, :, here] = part.reshape(chunks, rows, tile)
            return carry

        lax.fori_loop(0, samples // tile, sort, 0)
        fit(width, send * chunks, design_ref, target_ref, curve_ref, slope_ref, weight_ref)
        for chunk in range(chunks):
            out_ref[send * chunks + chunk] = spread_weights(
                weight_ref, chunk, width, count, curve_ref.shape[2] // width
            )

    for send in range(sends):

        def leave(k, carry):
            other = lax.rem(me + k, regions)
            copy(send, other, other).wait_send()
            return carry

        lax.fori_loop(1, regions, leave, 0)


def on_device(dosage, eigvec, eigval, pheno):
    samples, block = dosage.shape
    traits = pheno.shape[1]
    regions = lax.axis_size("region")
    ridges = len(HERITABILITY)
    per_device = traits // regions
    width = regions * ridges
    lanes = max(width, LANES)
    count = max(1, 2 * LANES // width)
    per_send = max(count, min(per_device, 2))
    sends = per_device // per_send
    chunks = per_send // count
    groups = per_send * width // lanes
    piece = per_send * ridges
    wire = jnp.bfloat16 if piece % 16 == 0 else jnp.float32
    vmem = pltpu.VMEM
    weights = pl.pallas_call(
        functools.partial(kernel, regions),
        out_shape=jax.ShapeDtypeStruct((sends * chunks, ROWS, count * width), jnp.float32),
        in_specs=[pl.BlockSpec(memory_space=vmem)] * 4,
        out_specs=pl.BlockSpec(memory_space=vmem),
        scratch_shapes=[
            vmem((samples, block), jnp.bfloat16),
            vmem((traits, samples), jnp.float32),
            vmem((traits, samples), jnp.bfloat16),
            vmem((traits, block), jnp.float32),
            vmem((traits * ridges, block), jnp.bfloat16),
            vmem((traits * ridges, block), jnp.bfloat16),
            vmem((traits * ridges, block), jnp.bfloat16),
            vmem((sends, regions, piece, samples), wire),
            vmem((sends, regions, piece, samples), wire),
            vmem((chunks, count * width, samples), jnp.bfloat16),
            vmem((sends * chunks, ROWS, samples), jnp.float32),
            vmem((groups, width, lanes), jnp.float32),
            vmem((groups, width, lanes), jnp.float32),
            vmem((groups, width, lanes), jnp.float32),
            pltpu.SemaphoreType.DMA((sends, regions)),
            pltpu.SemaphoreType.DMA((sends, regions)),
        ],
        compiler_params=pltpu.CompilerParams(
            collective_id=0, has_side_effects=True, vmem_limit_bytes=48 * 2**20
        ),
        name="stacked_ridge",
    )(dosage, eigvec, eigval, pheno)
    return jnp.sum(weights, axis=1).reshape(per_device, width)


def solution(mesh):
    return jax.shard_map(
        on_device,
        mesh=mesh,
        in_specs=(
            P("cohort", "region"),
            P("region", "cohort"),
            P("cohort", "region"),
            P("cohort", None),
        ),
        out_specs=P("region", "cohort"),
        check_vma=False,
    )
```

```python
import functools

import jax
import jax.numpy as jnp
from jax import lax
from jax.experimental import pallas as pl
from jax.experimental.pallas import tpu as pltpu
from jax.sharding import PartitionSpec as P

NEWTON = 3


EPSILON = 1e-05
HERITABILITY = (0.01, 0.25, 0.75, 0.99)
LEVEL_ONE = 0.03125
LANES = 128
ROWS = 8


def pick_column(matrix, column, width):
    lane = lax.broadcasted_iota(jnp.int32, matrix.shape, 1)
    if matrix.shape[1] == LANES:
        return jnp.take_along_axis(matrix, lane // width * width + column, axis=1)
    chosen = jnp.sum(jnp.where(lane == column, matrix, 0.0), axis=1, keepdims=True)
    return jnp.broadcast_to(chosen, matrix.shape)


def eliminate(curve_ref, slope_ref, width):
    groups = curve_ref.shape[0]
    lanes = curve_ref.shape[2]
    row = lax.broadcasted_iota(jnp.int32, (ROWS, lanes), 0)

    def panel(step, carry):
        first = pl.multiple_of(step * ROWS, ROWS)
        curves = [curve_ref[g, pl.ds(first, ROWS), :] for g in range(groups)]
        slopes = [slope_ref[g, pl.ds(first, ROWS), :] for g in range(groups)]
        for j in range(ROWS):
            for g in range(groups):
                column = pick_column(curves[g], first + j, width)
                inverse = 1.0 / column[j : j + 1, :]
                pivot = curves[g][j : j + 1, :] * inverse
                right = slopes[g][j : j + 1, :] * inverse
                curves[g] = jnp.where(row == j, pivot, curves[g] - column * pivot)
                slopes[g] = jnp.where(row == j, right, slopes[g] - column * right)
        for g in range(groups):
            old = curve_ref[g]
            curve = old
            slope = slope_ref[g]
            for j in range(ROWS):
                column = pick_column(old, first + j, width)
                curve = curve - column * curves[g][j : j + 1, :]
                slope = slope - column * slopes[g][j : j + 1, :]
            curve_ref[g] = curve
            slope_ref[g] = slope
        for g in range(groups):
            curve_ref[g, pl.ds(first, ROWS), :] = curves[g]
            slope_ref[g, pl.ds(first, ROWS), :] = slopes[g]
        return carry

    lax.fori_loop(0, width // ROWS, panel, 0)


def spread_weights(weight_ref, chunk, width, count, pack):
    lane = lax.broadcasted_iota(jnp.int32, (width, LANES), 1)
    parts = []
    for t in range(count):
        group, half = divmod(chunk * count + t, pack)
        held = weight_ref[group][:, :LANES]
        if half:
            held = pltpu.roll(held, LANES - half * width, 1)
        parts.append(jnp.where(lane == t, held, 0.0))
    return jnp.concatenate(parts, axis=0).T[:ROWS, :]


def fit(width, target_chunk, design_ref, target_ref, curve_ref, slope_ref, weight_ref):
    chunks, rows, samples = design_ref.shape
    count = rows // width
    lanes = curve_ref.shape[2]
    pack = lanes // width
    tile = 512
    ridge = LEVEL_ONE * samples
    weight_ref[...] = jnp.zeros_like(weight_ref)
    lane = lax.broadcasted_iota(jnp.int32, (width, lanes), 1)
    row = lax.broadcasted_iota(jnp.int32, (width, lanes), 0)
    identity = jnp.where(lane % width == row, ridge, 0.0)

    def newton(step, carry):
        for chunk in range(chunks):
            weights = spread_weights(weight_ref, chunk, width, count, pack).astype(jnp.bfloat16)
            gram = jnp.zeros((rows, rows), jnp.float32)
            grad = jnp.zeros((rows, ROWS), jnp.float32)
            for first in range(0, samples, tile):
                design = design_ref[chunk, :, first : first + tile]
                logits = jnp.dot(weights, design, preferred_element_type=jnp.float32)
                prob = 1.0 / (1.0 + jnp.exp(-logits))
                target = target_ref[target_chunk + chunk, :, first : first + tile]
                resid = (target - prob).astype(jnp.bfloat16)
                curve = prob * (1.0 - prob)
                weighted = jnp.concatenate(
                    [
                        (
                            design[t * width : (t + 1) * width].astype(jnp.float32)
                            * curve[t : t + 1, :]
                        ).astype(jnp.bfloat16)
                        for t in range(count)
                    ],
                    axis=0,
                )
                gram += dot_last(weighted, design)
                grad += dot_last(design, resid)
            for own in range(count // pack):
                group = chunk * count // pack + own
                curve = None
                for half in range(pack):
                    t = own * pack + half
                    part = gram[t * width : (t + 1) * width, own * lanes : (own + 1) * lanes]
                    side = jnp.broadcast_to(
                        grad[t * width : (t + 1) * width, t : t + 1], (width, lanes)
                    )
                    if curve is None:
                        curve, slope = part, side
                    else:
                        curve = jnp.where(lane < half * width, curve, part)
                        slope = jnp.where(lane < half * width, slope, side)
                curve_ref[group] = curve + identity
                slope_ref[group] = slope - ridge * weight_ref[group]
        eliminate(curve_ref, slope_ref, width)
        weight_ref[...] += slope_ref[...]
        return carry

    lax.fori_loop(0, NEWTON, newton, 0)


def dot_last(left, right):
    return lax.dot_general(
        left, right, (((1,), (1,)), ((), ())), preferred_element_type=jnp.float32
    )


def level_zero(
    regions,
    per_chunk,
    dosage_ref,
    eigvec_ref,
    eigval_ref,
    pheno_ref,
    *refs,
):
    *sent_refs, target_ref, geno_ref, trait_ref, std_trait_ref = refs[:-4]
    cross_ref, wide_ref, scaled_ref, ridge_ref = refs[-4:]
    samples, block = dosage_ref.shape
    traits = pheno_ref.shape[1]
    sends = len(sent_refs)
    _, piece, _ = sent_refs[0].shape
    ridges = len(HERITABILITY)
    count = per_chunk
    per_device = traits // regions
    per_send = per_device // sends
    tile = 256
    me = lax.axis_index("region")

    trait = pheno_ref[...].astype(jnp.float32).T
    trait_ref[...] = trait
    center = jnp.mean(trait, axis=1, keepdims=True)
    spread = jnp.sqrt(jnp.mean(jnp.square(trait - center), axis=1, keepdims=True) + EPSILON)
    std_trait_ref[...] = ((trait - center) / spread).astype(jnp.bfloat16)
    target_ref[...] = jnp.zeros_like(target_ref)
    for t in range(per_device):
        target_ref[t // count, t % count : t % count + 1, :] = trait_ref[
            pl.ds(me * per_device + t, 1), :
        ]

    def totals(i, carry):
        first, second = carry
        part = dosage_ref[pl.ds(pl.multiple_of(i * tile, tile), tile), :].astype(jnp.float32)
        part = part.reshape(tile // ROWS, ROWS, block)
        return first + jnp.sum(part, axis=0), second + jnp.sum(part * part, axis=0)

    zero = jnp.zeros((ROWS, block), jnp.float32)
    first, second = lax.fori_loop(0, samples // tile, totals, (zero, zero))
    first = jnp.sum(first, axis=0, keepdims=True)
    second = jnp.sum(second, axis=0, keepdims=True)
    mean = first / samples
    variance = (samples * second - first * first) / (samples * samples)
    scale = 1.0 / jnp.sqrt(variance + EPSILON)
    cross_ref[...] = jnp.zeros_like(cross_ref)

    def normalize(i, carry):
        here = pl.ds(pl.multiple_of(i * tile, tile), tile)
        part = ((dosage_ref[here, :].astype(jnp.float32) - mean) * scale).astype(jnp.bfloat16)
        geno_ref[here, :] = part
        cross_ref[...] += jnp.dot(
            std_trait_ref[:, here], part, preferred_element_type=jnp.float32
        )
        return carry

    lax.fori_loop(0, samples // tile, normalize, 0)

    all_rows = traits * ridges
    place = lax.broadcasted_iota(jnp.int32, (all_rows, traits), 0)
    which = lax.broadcasted_iota(jnp.int32, (all_rows, traits), 1)
    source = (
        place // piece % regions * per_device
        + place // (piece * regions) * per_send
        + place % per_send
    )
    choose = jnp.where(source == which, 1.0, 0.0).astype(jnp.bfloat16)
    wide_ref[...] = jnp.dot(
        choose, cross_ref[...].astype(jnp.bfloat16), preferred_element_type=jnp.float32
    ).astype(jnp.bfloat16)
    kind = lax.broadcasted_iota(jnp.int32, (all_rows, tile), 0) // per_send % ridges
    shrink = jnp.zeros((all_rows, tile), jnp.float32)
    for r, value in enumerate(HERITABILITY):
        shrink = jnp.where(kind == r, block * (1.0 - value) / value, shrink)

    def rotate(i, carry):
        here = pl.ds(pl.multiple_of(i * tile, tile), tile)
        rotated = jnp.dot(wide_ref[...], eigvec_ref[:, here], preferred_element_type=jnp.float32)
        scaled_ref[:, here] = (rotated / (eigval_ref[:, here] + shrink)).astype(jnp.bfloat16)
        return carry

    lax.fori_loop(0, block // tile, rotate, 0)

    def back(i, carry):
        here = pl.ds(pl.multiple_of(i * tile, tile), tile)
        ridge_ref[:, here] = dot_last(scaled_ref[...], eigvec_ref[here, :]).astype(jnp.bfloat16)
        return carry

    lax.fori_loop(0, block // tile, back, 0)

    send_rows = regions * piece
    for send in range(sends):

        def predict(i, carry):
            here = pl.ds(pl.multiple_of(i * tile, tile), tile)
            part = dot_last(
                ridge_ref[send * send_rows : (send + 1) * send_rows, :], geno_ref[here, :]
            )
            part = part.astype(jnp.bfloat16).astype(sent_refs[send].dtype)
            sent_refs[send][:, :, here] = part.reshape(regions, piece, tile)
            return carry

        lax.fori_loop(0, samples // tile, predict, 0)


def level_one(held_ref, target_ref, out_ref, design_ref, curve_ref, slope_ref, weight_ref):
    regions, piece, samples = held_ref.shape
    chunks, rows, _ = design_ref.shape
    ridges = len(HERITABILITY)
    width = regions * ridges
    per_send = piece // ridges
    send_rows = regions * piece
    tile = 256
    place = lax.broadcasted_iota(jnp.int32, (send_rows, send_rows), 0)
    which = lax.broadcasted_iota(jnp.int32, (send_rows, send_rows), 1)
    wanted = which % per_send * width + which // per_send % ridges * regions + which // piece
    order = jnp.where(place == wanted, 1.0, 0.0).astype(jnp.bfloat16)

    def sort(i, carry):
        here = pl.ds(pl.multiple_of(i * tile, tile), tile)
        part = held_ref[:, :, here].reshape(send_rows, tile).astype(jnp.bfloat16)
        part = jnp.dot(order, part, preferred_element_type=jnp.float32).astype(jnp.bfloat16)
        design_ref[:, :, here] = part.reshape(chunks, rows, tile)
        return carry

    lax.fori_loop(0, samples // tile, sort, 0)
    fit(width, 0, design_ref, target_ref, curve_ref, slope_ref, weight_ref)
    for chunk in range(chunks):
        out_ref[chunk] = spread_weights(
            weight_ref, chunk, width, rows // width, curve_ref.shape[2] // width
        )


def on_device(dosage, eigvec, eigval, pheno):
    samples, block = dosage.shape
    traits = pheno.shape[1]
    regions = lax.axis_size("region")
    ridges = len(HERITABILITY)
    per_device = traits // regions
    width = regions * ridges
    lanes = max(width, LANES)
    count = max(1, 2 * LANES // width)
    per_send = max(count, min(per_device, 2))
    sends = per_device // per_send
    chunks = per_send // count
    groups = per_send * width // lanes
    piece = per_send * ridges
    wire = jnp.bfloat16 if piece % 16 == 0 else jnp.float32
    vmem = pltpu.VMEM
    in_vmem = pl.BlockSpec(memory_space=vmem)
    params = pltpu.CompilerParams(vmem_limit_bytes=40 * 2**20)
    *sent, target = pl.pallas_call(
        functools.partial(level_zero, regions, count),
        out_shape=[
            *[jax.ShapeDtypeStruct((regions, piece, samples), wire)] * sends,
            jax.ShapeDtypeStruct((sends * chunks, ROWS, samples), jnp.float32),
        ],
        in_specs=[in_vmem] * 4,
        out_specs=[in_vmem] * (sends + 1),
        scratch_shapes=[
            vmem((samples, block), jnp.bfloat16),
            vmem((traits, samples), jnp.float32),
            vmem((traits, samples), jnp.bfloat16),
            vmem((traits, block), jnp.float32),
            vmem((traits * ridges, block), jnp.bfloat16),
            vmem((traits * ridges, block), jnp.bfloat16),
            vmem((traits * ridges, block), jnp.bfloat16),
        ],
        compiler_params=params,
        name="level_zero",
    )(dosage, eigvec, eigval, pheno)
    held = [
        lax.all_to_all(sent[send], "region", split_axis=0, concat_axis=0, tiled=True)
        for send in range(sends)
    ]
    weights = [
        pl.pallas_call(
            level_one,
            out_shape=jax.ShapeDtypeStruct((chunks, ROWS, count * width), jnp.float32),
            in_specs=[in_vmem] * 2,
            out_specs=in_vmem,
            scratch_shapes=[
                vmem((chunks, count * width, samples), jnp.bfloat16),
                vmem((groups, width, lanes), jnp.float32),
                vmem((groups, width, lanes), jnp.float32),
                vmem((groups, width, lanes), jnp.float32),
            ],
            compiler_params=params,
            cost_estimate=pl.CostEstimate(
                flops=20_000_000_000, bytes_accessed=2**20, transcendentals=0
            ),
            name="level_one",
        )(held[send], target[send * chunks : (send + 1) * chunks])
        for send in range(sends)
    ]
    return jnp.sum(jnp.concatenate(weights), axis=1).reshape(per_device, width)


def solution(mesh):
    return jax.shard_map(
        on_device,
        mesh=mesh,
        in_specs=(
            P("cohort", "region"),
            P("region", "cohort"),
            P("cohort", "region"),
            P("cohort", None),
        ),
        out_specs=P("region", "cohort"),
        check_vma=False,
    )
```

```python
import functools

import jax
import jax.numpy as jnp
from jax import lax
from jax.experimental import pallas as pl
from jax.experimental.pallas import tpu as pltpu
from jax.sharding import PartitionSpec as P

NEWTON = 3


EPSILON = 1e-05
HERITABILITY = (0.01, 0.25, 0.75, 0.99)
LEVEL_ONE = 0.03125
LANES = 128
ROWS = 8


def pick_column(matrix, column, width):
    lane = lax.broadcasted_iota(jnp.int32, matrix.shape, 1)
    if matrix.shape[1] == LANES:
        return jnp.take_along_axis(matrix, lane // width * width + column, axis=1)
    chosen = jnp.sum(jnp.where(lane == column, matrix, 0.0), axis=1, keepdims=True)
    return jnp.broadcast_to(chosen, matrix.shape)


def eliminate(curve_ref, slope_ref, width):
    groups = curve_ref.shape[0]
    lanes = curve_ref.shape[2]
    row = lax.broadcasted_iota(jnp.int32, (ROWS, lanes), 0)

    def panel(step, carry):
        first = pl.multiple_of(step * ROWS, ROWS)
        curves = [curve_ref[g, pl.ds(first, ROWS), :] for g in range(groups)]
        slopes = [slope_ref[g, pl.ds(first, ROWS), :] for g in range(groups)]
        for j in range(ROWS):
            for g in range(groups):
                column = pick_column(curves[g], first + j, width)
                inverse = pl.reciprocal(column[j : j + 1, :], approx=True)
                inverse = inverse * (2.0 - column[j : j + 1, :] * inverse)
                inverse = inverse * (2.0 - column[j : j + 1, :] * inverse)
                pivot = curves[g][j : j + 1, :] * inverse
                right = slopes[g][j : j + 1, :] * inverse
                curves[g] = jnp.where(row == j, pivot, curves[g] - column * pivot)
                slopes[g] = jnp.where(row == j, right, slopes[g] - column * right)
        for g in range(groups):
            old = curve_ref[g]
            curve = old
            slope = slope_ref[g]
            for j in range(ROWS):
                column = pick_column(old, first + j, width)
                curve = curve - column * curves[g][j : j + 1, :]
                slope = slope - column * slopes[g][j : j + 1, :]
            curve_ref[g] = curve
            slope_ref[g] = slope
        for g in range(groups):
            curve_ref[g, pl.ds(first, ROWS), :] = curves[g]
            slope_ref[g, pl.ds(first, ROWS), :] = slopes[g]
        return carry

    lax.fori_loop(0, width // ROWS, panel, 0)


def spread_weights(weight_ref, chunk, width, count, pack):
    lane = lax.broadcasted_iota(jnp.int32, (width, LANES), 1)
    parts = []
    for t in range(count):
        group, half = divmod(chunk * count + t, pack)
        held = weight_ref[group][:, :LANES]
        if half:
            held = pltpu.roll(held, LANES - half * width, 1)
        parts.append(jnp.where(lane == t, held, 0.0))
    return jnp.concatenate(parts, axis=0).T[:ROWS, :]


def fit(width, target_chunk, design_ref, target_ref, curve_ref, slope_ref, weight_ref):
    chunks, rows, samples = design_ref.shape
    count = rows // width
    lanes = curve_ref.shape[2]
    pack = lanes // width
    tile = 512
    ridge = LEVEL_ONE * samples
    weight_ref[...] = jnp.zeros_like(weight_ref)
    lane = lax.broadcasted_iota(jnp.int32, (width, lanes), 1)
    row = lax.broadcasted_iota(jnp.int32, (width, lanes), 0)
    identity = jnp.where(lane % width == row, ridge, 0.0)

    def newton(step, carry):
        for chunk in range(chunks):
            weights = spread_weights(weight_ref, chunk, width, count, pack).astype(jnp.bfloat16)
            gram = jnp.zeros((rows, rows), jnp.float32)
            grad = jnp.zeros((rows, ROWS), jnp.float32)
            for first in range(0, samples, tile):
                design = design_ref[chunk, :, first : first + tile]
                logits = jnp.dot(weights, design, preferred_element_type=jnp.float32)
                prob = 1.0 / (1.0 + jnp.exp(-logits))
                target = target_ref[target_chunk + chunk, :, first : first + tile]
                resid = (target - prob).astype(jnp.bfloat16)
                curve = prob * (1.0 - prob)
                weighted = jnp.concatenate(
                    [
                        (
                            design[t * width : (t + 1) * width].astype(jnp.float32)
                            * curve[t : t + 1, :]
                        ).astype(jnp.bfloat16)
                        for t in range(count)
                    ],
                    axis=0,
                )
                gram += dot_last(weighted, design)
                grad += dot_last(design, resid)
            for own in range(count // pack):
                group = chunk * count // pack + own
                curve = None
                for half in range(pack):
                    t = own * pack + half
                    part = gram[t * width : (t + 1) * width, own * lanes : (own + 1) * lanes]
                    side = jnp.broadcast_to(
                        grad[t * width : (t + 1) * width, t : t + 1], (width, lanes)
                    )
                    if curve is None:
                        curve, slope = part, side
                    else:
                        curve = jnp.where(lane < half * width, curve, part)
                        slope = jnp.where(lane < half * width, slope, side)
                curve_ref[group] = curve + identity
                slope_ref[group] = slope - ridge * weight_ref[group]
        eliminate(curve_ref, slope_ref, width)
        weight_ref[...] += slope_ref[...]
        return carry

    lax.fori_loop(0, NEWTON, newton, 0)


def dot_last(left, right):
    return lax.dot_general(
        left, right, (((1,), (1,)), ((), ())), preferred_element_type=jnp.float32
    )


def level_zero(
    regions,
    per_chunk,
    dosage_ref,
    eigvec_ref,
    eigval_ref,
    pheno_ref,
    *refs,
):
    *sent_refs, target_ref, geno_ref, trait_ref, std_trait_ref = refs[:-4]
    cross_ref, wide_ref, scaled_ref, ridge_ref = refs[-4:]
    samples, block = dosage_ref.shape
    traits = pheno_ref.shape[1]
    sends = len(sent_refs)
    _, piece, _ = sent_refs[0].shape
    ridges = len(HERITABILITY)
    count = per_chunk
    per_device = traits // regions
    per_send = per_device // sends
    tile = 256
    me = lax.axis_index("region")

    trait = pheno_ref[...].astype(jnp.float32).T
    trait_ref[...] = trait
    center = jnp.mean(trait, axis=1, keepdims=True)
    spread = jnp.sqrt(jnp.mean(jnp.square(trait - center), axis=1, keepdims=True) + EPSILON)
    std_trait_ref[...] = ((trait - center) / spread).astype(jnp.bfloat16)
    target_ref[...] = jnp.zeros_like(target_ref)
    for t in range(per_device):
        target_ref[t // count, t % count : t % count + 1, :] = trait_ref[
            pl.ds(me * per_device + t, 1), :
        ]

    def totals(i, carry):
        first, second = carry
        part = dosage_ref[pl.ds(pl.multiple_of(i * tile, tile), tile), :].astype(jnp.float32)
        part = part.reshape(tile // ROWS, ROWS, block)
        return first + jnp.sum(part, axis=0), second + jnp.sum(part * part, axis=0)

    zero = jnp.zeros((ROWS, block), jnp.float32)
    first, second = lax.fori_loop(0, samples // tile, totals, (zero, zero))
    first = jnp.sum(first, axis=0, keepdims=True)
    second = jnp.sum(second, axis=0, keepdims=True)
    mean = first / samples
    variance = (samples * second - first * first) / (samples * samples)
    scale = 1.0 / jnp.sqrt(variance + EPSILON)
    cross_ref[...] = jnp.zeros_like(cross_ref)

    def normalize(i, carry):
        here = pl.ds(pl.multiple_of(i * tile, tile), tile)
        part = ((dosage_ref[here, :].astype(jnp.float32) - mean) * scale).astype(jnp.bfloat16)
        geno_ref[here, :] = part
        cross_ref[...] += jnp.dot(
            std_trait_ref[:, here], part, preferred_element_type=jnp.float32
        )
        return carry

    lax.fori_loop(0, samples // tile, normalize, 0)

    all_rows = traits * ridges
    place = lax.broadcasted_iota(jnp.int32, (all_rows, traits), 0)
    which = lax.broadcasted_iota(jnp.int32, (all_rows, traits), 1)
    source = (
        place // piece % regions * per_device
        + place // (piece * regions) * per_send
        + place % per_send
    )
    choose = jnp.where(source == which, 1.0, 0.0).astype(jnp.bfloat16)
    wide_ref[...] = jnp.dot(
        choose, cross_ref[...].astype(jnp.bfloat16), preferred_element_type=jnp.float32
    ).astype(jnp.bfloat16)
    kind = lax.broadcasted_iota(jnp.int32, (all_rows, tile), 0) // per_send % ridges
    shrink = jnp.zeros((all_rows, tile), jnp.float32)
    for r, value in enumerate(HERITABILITY):
        shrink = jnp.where(kind == r, block * (1.0 - value) / value, shrink)

    def rotate(i, carry):
        here = pl.ds(pl.multiple_of(i * tile, tile), tile)
        rotated = jnp.dot(wide_ref[...], eigvec_ref[:, here], preferred_element_type=jnp.float32)
        scaled_ref[:, here] = (rotated / (eigval_ref[:, here] + shrink)).astype(jnp.bfloat16)
        return carry

    lax.fori_loop(0, block // tile, rotate, 0)

    def back(i, carry):
        here = pl.ds(pl.multiple_of(i * tile, tile), tile)
        ridge_ref[:, here] = dot_last(scaled_ref[...], eigvec_ref[here, :]).astype(jnp.bfloat16)
        return carry

    lax.fori_loop(0, block // tile, back, 0)

    send_rows = regions * piece
    for send in range(sends):

        def predict(i, carry):
            here = pl.ds(pl.multiple_of(i * tile, tile), tile)
            part = dot_last(
                ridge_ref[send * send_rows : (send + 1) * send_rows, :], geno_ref[here, :]
            )
            part = part.astype(jnp.bfloat16).astype(sent_refs[send].dtype)
            sent_refs[send][:, :, here] = part.reshape(regions, piece, tile)
            return carry

        lax.fori_loop(0, samples // tile, predict, 0)


def level_one(held_ref, target_ref, out_ref, design_ref, curve_ref, slope_ref, weight_ref):
    regions, piece, samples = held_ref.shape
    chunks, rows, _ = design_ref.shape
    ridges = len(HERITABILITY)
    width = regions * ridges
    per_send = piece // ridges
    send_rows = regions * piece
    tile = 256
    place = lax.broadcasted_iota(jnp.int32, (send_rows, send_rows), 0)
    which = lax.broadcasted_iota(jnp.int32, (send_rows, send_rows), 1)
    wanted = which % per_send * width + which // per_send % ridges * regions + which // piece
    order = jnp.where(place == wanted, 1.0, 0.0).astype(jnp.bfloat16)

    def sort(i, carry):
        here = pl.ds(pl.multiple_of(i * tile, tile), tile)
        part = held_ref[:, :, here].reshape(send_rows, tile).astype(jnp.bfloat16)
        part = jnp.dot(order, part, preferred_element_type=jnp.float32).astype(jnp.bfloat16)
        design_ref[:, :, here] = part.reshape(chunks, rows, tile)
        return carry

    lax.fori_loop(0, samples // tile, sort, 0)
    fit(width, 0, design_ref, target_ref, curve_ref, slope_ref, weight_ref)
    for chunk in range(chunks):
        out_ref[chunk] = spread_weights(
            weight_ref, chunk, width, rows // width, curve_ref.shape[2] // width
        )


def on_device(dosage, eigvec, eigval, pheno):
    samples, block = dosage.shape
    traits = pheno.shape[1]
    regions = lax.axis_size("region")
    ridges = len(HERITABILITY)
    per_device = traits // regions
    width = regions * ridges
    lanes = max(width, LANES)
    count = max(1, 2 * LANES // width)
    per_send = per_device
    sends = per_device // per_send
    chunks = per_send // count
    groups = per_send * width // lanes
    piece = per_send * ridges
    wire = jnp.bfloat16 if piece % 16 == 0 else jnp.float32
    vmem = pltpu.VMEM
    in_vmem = pl.BlockSpec(memory_space=vmem)
    params = pltpu.CompilerParams(vmem_limit_bytes=40 * 2**20)
    *sent, target = pl.pallas_call(
        functools.partial(level_zero, regions, count),
        out_shape=[
            *[jax.ShapeDtypeStruct((regions, piece, samples), wire)] * sends,
            jax.ShapeDtypeStruct((sends * chunks, ROWS, samples), jnp.float32),
        ],
        in_specs=[in_vmem] * 4,
        out_specs=[in_vmem] * (sends + 1),
        scratch_shapes=[
            vmem((samples, block), jnp.bfloat16),
            vmem((traits, samples), jnp.float32),
            vmem((traits, samples), jnp.bfloat16),
            vmem((traits, block), jnp.float32),
            vmem((traits * ridges, block), jnp.bfloat16),
            vmem((traits * ridges, block), jnp.bfloat16),
            vmem((traits * ridges, block), jnp.bfloat16),
        ],
        compiler_params=params,
        name="level_zero",
    )(dosage, eigvec, eigval, pheno)
    held = [
        lax.all_to_all(sent[send], "region", split_axis=0, concat_axis=0, tiled=True)
        for send in range(sends)
    ]
    weights = [
        pl.pallas_call(
            level_one,
            out_shape=jax.ShapeDtypeStruct((chunks, ROWS, count * width), jnp.float32),
            in_specs=[in_vmem] * 2,
            out_specs=in_vmem,
            scratch_shapes=[
                vmem((chunks, count * width, samples), jnp.bfloat16),
                vmem((groups, width, lanes), jnp.float32),
                vmem((groups, width, lanes), jnp.float32),
                vmem((groups, width, lanes), jnp.float32),
            ],
            compiler_params=params,
            cost_estimate=pl.CostEstimate(
                flops=20_000_000_000, bytes_accessed=2**20, transcendentals=0
            ),
            name="level_one",
        )(held[send], target[send * chunks : (send + 1) * chunks])
        for send in range(sends)
    ]
    return jnp.sum(jnp.concatenate(weights), axis=1).reshape(per_device, width)


def solution(mesh):
    return jax.shard_map(
        on_device,
        mesh=mesh,
        in_specs=(
            P("cohort", "region"),
            P("region", "cohort"),
            P("cohort", "region"),
            P("cohort", None),
        ),
        out_specs=P("region", "cohort"),
        check_vma=False,
    )
```
